32 devices in a mesh: groups: 2 (over y), row: 4 (over z), col: 4 (over x, core).
Axes of the slice: x: 2, y: 2, z: 4, core: 2. Of those that a mesh axis runs over, the one named last changes fastest.
Arguments:
- hidden: bfloat16 [2048, 8192], P(('groups', 'col'), 'row'), parts along dimension 0, may hold values from -6 to 6
- grad_out: bfloat16 [2048, 4096], P(('groups', 'row'), 'col'), parts along dimension 0, may hold values from -6 to 6
- example_ids: int32 [2048], P(('groups', 'col')), parts along dimension 0, may hold values from 0 to 1, never falling along the last dimension, each value on 1 to 768 neighbouring positions
- sign_bits: int32 [8192, 4096], P('row', 'col'), may hold values from 0 to 1
- sample_index: int32 [8192], replicated, may hold values from 0 to 33554431
Outputs:
- projections: float32 [4, 8192], P('groups', ('row', 'col')), parts along dimension 0
The draws below stay inside these ranges and needn't reach their ends.
There are 2 independent parts, one for each index of `groups`. The reference program is written for one: setup_inputs(seed, part) draws one part's arguments, and reference() takes and returns one part's arrays. A program takes and returns all parts, laid end to end along the dimension named above; an argument that names none is the same for every part. Nothing has to cross between parts.
Inputs may be any that keep to these rules, and one draw needn't show every extreme that they name: `example_ids`: example ids never fall along the tokens; every example has at least one token.
All inputs are finite; a program needn't handle non-finite values.
Results may differ from the reference program's by a relative error of at most 0.0003.
Values may be sent and summed in bfloat16 or wider, within the bound.
A program may use at most 320 MiB of HBM per device.

```python
import math
import jax
import jax.numpy as jnp
import numpy as np
from jax import lax

D = 4096
FFW = 8192
EXAMPLES = 2
TOK_EX = 512
SAMPLES = 8192
TOKENS = 1024
HAD = 33554432


def set_ends(values, stream_key, least, high):
    extent = values.shape
    place = [jax.random.randint(jax.random.fold_in(stream_key, axis), (), 0, extent[axis]) for axis in range(len(extent))]
    values = values.at[tuple(place)].set(least)
    longest = extent.index(max(extent))
    place[longest] = (place[longest] + 1) % extent[longest]
    return values.at[tuple(place)].set(high)


def steps_of(own_key, extent, cuts, least, top_value):
    loudness, own = 1.0, jax.random.fold_in(own_key, 6)
    for position, parts in cuts:
        draws = jnp.exp(jax.random.uniform(jax.random.fold_in(own, position), (parts,), jnp.float32, least / len(cuts), top_value / len(cuts)))
        loudness = loudness * jnp.repeat(draws, extent[position] // parts).reshape([-1 if axis == position else 1 for axis in range(len(extent))])
    return loudness


def profile(count, total, reach, slope):
    portions = [(1 << 20) // math.isqrt(rank ** slope) + 1 for rank in range(2, count + 1)]
    spare, holding = total - reach - (count - 1), [1] * (count - 1)
    while spare > 0:
        free = [i for i in range(count - 1) if holding[i] < reach]
        pool, budget = sum([portions[i] for i in free]), spare
        for i in free:
            more = min(reach - holding[i], max(1, budget * portions[i] // pool), spare)
            holding[i] = holding[i] + more
            spare = spare - more
    return np.array([reach] + holding)


def ragged_sizes(rng, amount, total, most, slope):
    if amount == 2:
        one = jax.random.randint(rng, (), max(1, total - most), min(most, total - 1) + 1)
        return jnp.stack([one, total - one])
    sizes = jnp.asarray(profile(amount, total, most, slope), jnp.int32)
    couples = (amount - 1) // 2
    source_of, receiver = sizes[1:1 + 2 * couples:2], sizes[2:2 + 2 * couples:2]
    slack = jnp.minimum(source_of - 1, most - receiver)
    shifted = jax.random.randint(jax.random.fold_in(rng, 1), (couples,), 0, 1 << 20) % (slack + 1)
    sizes = sizes.at[1:1 + 2 * couples:2].set(source_of - shifted).at[2:2 + 2 * couples:2].set(receiver + shifted)
    return sizes[jax.random.permutation(jax.random.fold_in(rng, 2), amount)]


def noise(stream_key, shape, spread, bound, pieces=(), kind=jnp.bfloat16):
    factor_of = steps_of(stream_key, shape, pieces, -0.22, 0.18) if pieces else 1.0
    entries = jax.random.normal(stream_key, shape, jnp.float32) * spread * factor_of
    return jnp.minimum(jnp.maximum(entries, -bound), bound).astype(kind)


def setup_inputs(seed: int = 0, part: int = 0) -> dict:
    seeds = jax.random.split(jax.random.key(seed), 6)
    part_splits = jax.random.split(jax.random.fold_in(seeds[5], part), 6)
    return {
        "hidden": noise(part_splits[0], (TOKENS, FFW), 1.0, 6.0, ((0, 4), (1, 4))),
        "grad_out": noise(part_splits[1], (TOKENS, D), 1.0, 6.0, ((0, 4), (1, 4))),
        "example_ids": jnp.searchsorted(jnp.cumsum(ragged_sizes(part_splits[2], EXAMPLES, TOKENS, TOK_EX + TOK_EX // 2, 0)), jnp.arange(TOKENS), side="right").astype(jnp.int32),
        "sign_bits": set_ends(jax.random.randint(seeds[3], (FFW, D), 0, 2), jax.random.fold_in(seeds[3], 1), 0, 1).astype(jnp.int32),
        "sample_index": set_ends(jax.random.randint(seeds[4], (SAMPLES,), 0, HAD), jax.random.fold_in(seeds[4], 1), 0, HAD - 1).astype(jnp.int32),
    }


def transform_flat(vector):
    length = vector.shape[0]
    for level in range(length.bit_length() - 1):
        shaped = vector.reshape(-1, 2, 2 ** level)
        vector = jnp.stack((shaped[:, 0] + shaped[:, 1], shaped[:, 0] - shaped[:, 1]), axis=1).reshape(-1)
    return vector

def reference(hidden, grad_out, example_ids, sign_bits, sample_index):
    scale = 1.0 / math.sqrt(FFW * D * TOK_EX)
    hidden_wide = hidden.astype(jnp.float32)
    grads_wide = grad_out.astype(jnp.float32)
    signs = (1 - 2 * sign_bits).astype(jnp.float32)

    def one_example(example):
        weight = (example_ids == example).astype(jnp.float32)
        grads = jnp.dot((hidden_wide * weight[:, None]).T, grads_wide, precision=lax.Precision.HIGHEST)
        flipped = grads * signs * scale
        transformed = transform_flat(flipped.reshape(-1))
        return transformed[sample_index]
    return lax.map(one_example, jnp.arange(EXAMPLES, dtype=jnp.int32))
```

```python
import functools
import math

import jax
import jax.numpy as jnp
import numpy as np
from jax import lax
from jax.experimental import pallas as pl
from jax.experimental.pallas import tpu as pltpu
from jax.sharding import PartitionSpec as P

EXAMPLES = 2
TOK_EX = 512
LANES = 128
WIDE = 256
UNROLL = 16
BATCH = 1024


def sylvester(order):
    table = np.ones((1, 1), np.float32)
    while table.shape[0] < order:
        table = np.block([[table, table], [table, -table]])
    return jnp.asarray(table, jnp.bfloat16)


def butterfly(values):
    span = 1
    values = list(values)
    while span < len(values):
        for start in range(0, len(values), 2 * span):
            for i in range(start, start + span):
                a, b = values[i], values[i + span]
                values[i], values[i + span] = a + b, a - b
        span *= 2
    return values


def split(values):
    high = values.astype(jnp.bfloat16)
    return high, (values - high.astype(jnp.float32)).astype(jnp.bfloat16)


def kernel(
    order, place_ref, ids_ref, low_ref, hidden_ref, grad_ref, sign_ref, pair_ref, lane_ref,
    out_ref, table, flipped, parts, picked,
):
    step = pl.program_id(0)
    rows = hidden_ref.shape[0]
    blocks = rows // order
    chunks = table.shape[1]
    samples = low_ref.shape[1]

    labels = ids_ref[...]
    for e in range(EXAMPLES):
        masked = jnp.where(labels == e, grad_ref[...].astype(jnp.float32), 0.0).astype(jnp.bfloat16)

        def multiply(b, _):
            at = pl.ds(pl.multiple_of(b * order, order), order)
            grads = jnp.dot(hidden_ref[at, :], masked, preferred_element_type=jnp.float32)
            flipped[b] = jnp.where(sign_ref[at, :] == 0, grads, -grads)
            return 0

        lax.fori_loop(0, blocks, multiply, 0)

        def mix(i, _):
            at = pl.ds(pl.multiple_of(i * 16, 16), 16)
            below = pl.ds(pl.multiple_of(order + i * 16, 16), 16)
            values = butterfly([flipped[b, at, :] for b in range(blocks)])
            for b in range(blocks):
                high, low = split(values[b])
                parts[b, at, :] = high
                parts[b, below, :] = low
            return 0

        lax.fori_loop(0, order // 16, mix, 0)

        def transform(b, _):
            at = pl.ds(pl.multiple_of(b * order, order), order)
            values = jnp.dot(pair_ref[...], parts[b], preferred_element_type=jnp.float32)
            for half in range(WIDE // LANES):
                table[e, step * (WIDE // LANES) + half, at, :] = values[:, half * LANES:(half + 1) * LANES]
            return 0

        lax.fori_loop(0, blocks, transform, 0)

    @pl.when(step == pl.num_programs(0) - 1)
    def _():
        for e in range(EXAMPLES):
            def across(i, _):
                at = pl.ds(pl.multiple_of(i * 16, 16), 16)
                values = butterfly([table[e, c, at, :] for c in range(chunks)])
                for c in range(chunks):
                    table[e, c, at, :] = values[c]
                return 0

            lax.fori_loop(0, rows // 16, across, 0)

        flat = table.reshape(EXAMPLES, chunks * rows, LANES)
        lane = lax.broadcasted_iota(jnp.int32, (LANES, BATCH), 0)

        def sample(n, _):
            base = n * BATCH

            def pick(i, _):
                for u in range(UNROLL):
                    k = i * UNROLL + u
                    place = place_ref[base + k]
                    for e in range(EXAMPLES):
                        picked[e, pl.ds(k, 1), :] = flat[e, pl.ds(place, 1), :]
                return 0

            lax.fori_loop(0, BATCH // UNROLL, pick, 0)
            at = pl.ds(pl.multiple_of(base, BATCH), BATCH)
            keep = lane == low_ref[:, at]
            for e in range(EXAMPLES):
                high, low = split(picked[e])
                dims = (((1,), (1,)), ((), ()))
                values = lax.dot_general(lane_ref[...], high, dims, preferred_element_type=jnp.float32)
                values = values + lax.dot_general(lane_ref[...], low, dims, preferred_element_type=jnp.float32)
                out_ref[e:e + 1, at] = jnp.sum(jnp.where(keep, values, 0.0), axis=0, keepdims=True)
            return 0

        lax.fori_loop(0, samples // BATCH, sample, 0)


def sketch(hidden, grad, ids, sign_bits, place, low):
    rows, tokens = hidden.shape
    columns = grad.shape[1]
    order = min(rows, 256)
    chunks = columns // LANES
    whole = lambda j, place: (0, 0)
    half = sylvester(order)
    return pl.pallas_call(
        functools.partial(kernel, order),
        out_shape=jax.ShapeDtypeStruct((EXAMPLES, low.shape[1]), jnp.float32),
        grid_spec=pltpu.PrefetchScalarGridSpec(
            num_scalar_prefetch=1,
            grid=(columns // WIDE,),
            in_specs=[
                pl.BlockSpec((tokens, 1), whole),
                pl.BlockSpec((1, low.shape[1]), whole),
                pl.BlockSpec((rows, tokens), whole),
                pl.BlockSpec((tokens, WIDE), lambda j, place: (0, j)),
                pl.BlockSpec((rows, WIDE), lambda j, place: (0, j)),
                pl.BlockSpec((order, 2 * order), whole),
                pl.BlockSpec((LANES, LANES), whole),
            ],
            out_specs=pl.BlockSpec((EXAMPLES, low.shape[1]), whole),
            scratch_shapes=[
                pltpu.VMEM((EXAMPLES, chunks, rows, LANES), jnp.float32),
                pltpu.VMEM((rows // order, order, WIDE), jnp.float32),
                pltpu.VMEM((rows // order, 2 * order, WIDE), jnp.bfloat16),
                pltpu.VMEM((EXAMPLES, BATCH, LANES), jnp.float32),
            ],
        ),
        compiler_params=pltpu.CompilerParams(vmem_limit_bytes=56 << 20),
        name="sketch",
    )(place, ids, low, hidden, grad, sign_bits, jnp.concatenate([half, half], axis=1), sylvester(LANES))


def shards(hidden, grad_out, example_ids, sign_bits, sample_index):
    row_block = hidden.shape[1]
    col_block = grad_out.shape[1]
    row_count = lax.axis_size("row")
    col_count = lax.axis_size("col")
    d_total = col_block * col_count
    grad_all = lax.all_gather(grad_out, "row", axis=0, tiled=True)
    hidden_all = lax.all_gather(hidden.T, "col", axis=1, tiled=True)
    ids = lax.all_gather(example_ids, "col", axis=0, tiled=True)
    row_global = sample_index // d_total
    col_global = sample_index % d_total
    row_inner = row_global % row_block
    col_inner = col_global % col_block
    place = (col_inner // LANES) * row_block + row_inner
    low = (col_inner % LANES)[None, :]
    common = jnp.bitwise_count((row_global // row_block) & lax.axis_index("row"))
    common += jnp.bitwise_count((col_global // col_block) & lax.axis_index("col"))
    scale = 1.0 / math.sqrt(row_block * row_count * d_total * TOK_EX)
    weight = jnp.where(common % 2 == 0, scale, -scale).astype(jnp.float32)
    terms = sketch(hidden_all, grad_all, ids[:, None], sign_bits, place, low) * weight[None, :]
    return lax.psum_scatter(terms, ("row", "col"), scatter_dimension=1, tiled=True)


def solution(mesh):
    placed = (
        P(("groups", "col"), "row"),
        P(("groups", "row"), "col"),
        P(("groups", "col")),
        P("row", "col"),
        P(),
    )
    return jax.shard_map(
        shards, mesh=mesh, in_specs=placed, out_specs=P("groups", ("row", "col")), check_vma=False
    )
```

```python
import functools
import math

import jax
import jax.numpy as jnp
import numpy as np
from jax import lax
from jax.experimental import pallas as pl
from jax.experimental.pallas import tpu as pltpu
from jax.sharding import PartitionSpec as P

EXAMPLES = 2
TOK_EX = 512
LANES = 128
WIDE = 256
UNROLL = 16
BATCH = 1024
PIECES = 4
MESH = pl.DeviceIdType.MESH


def sylvester(order):
    table = np.ones((1, 1), np.float32)
    while table.shape[0] < order:
        table = np.block([[table, table], [table, -table]])
    return jnp.asarray(table, jnp.bfloat16)


def butterfly(values):
    span = 1
    values = list(values)
    while span < len(values):
        for start in range(0, len(values), 2 * span):
            for i in range(start, start + span):
                a, b = values[i], values[i + span]
                values[i], values[i + span] = a + b, a - b
        span *= 2
    return values


def split(values):
    high = values.astype(jnp.bfloat16)
    return high, (values - high.astype(jnp.float32)).astype(jnp.bfloat16)


def kernel(
    order, place_ref, ids_ref, low_ref, hidden_ref, grad_ref, sign_ref, pair_ref, lane_ref,
    out_ref, table, flipped, parts, picked,
):
    step = pl.program_id(0)
    rows = hidden_ref.shape[0]
    blocks = rows // order
    chunks = table.shape[1]
    samples = low_ref.shape[1]

    labels = jnp.concatenate([ids_ref[...]] * (WIDE // LANES), axis=1).astype(jnp.float32)
    for e in range(EXAMPLES):
        masked = jnp.where(labels == e, grad_ref[...].astype(jnp.float32), 0.0).astype(jnp.bfloat16)

        def multiply(b, _):
            at = pl.ds(pl.multiple_of(b * order, order), order)
            grads = jnp.dot(hidden_ref[at, :], masked, preferred_element_type=jnp.float32)
            flipped[b] = jnp.where(sign_ref[at, :] == 0, grads, -grads)
            return 0

        lax.fori_loop(0, blocks, multiply, 0)

        def mix(i, _):
            at = pl.ds(pl.multiple_of(i * 16, 16), 16)
            below = pl.ds(pl.multiple_of(order + i * 16, 16), 16)
            values = butterfly([flipped[b, at, :] for b in range(blocks)])
            for b in range(blocks):
                high, low = split(values[b])
                parts[b, at, :] = high
                parts[b, below, :] = low
            return 0

        lax.fori_loop(0, order // 16, mix, 0)

        def transform(b, _):
            at = pl.ds(pl.multiple_of(b * order, order), order)
            values = jnp.dot(pair_ref[...], parts[b], preferred_element_type=jnp.float32)
            for half in range(WIDE // LANES):
                table[e, step * (WIDE // LANES) + half, at, :] = values[:, half * LANES:(half + 1) * LANES]
            return 0

        lax.fori_loop(0, blocks, transform, 0)

    @pl.when(step == pl.num_programs(0) - 1)
    def _():
        for e in range(EXAMPLES):
            def across(i, _):
                at = pl.ds(pl.multiple_of(i * 16, 16), 16)
                values = butterfly([table[e, c, at, :] for c in range(chunks)])
                for c in range(chunks):
                    table[e, c, at, :] = values[c]
                return 0

            lax.fori_loop(0, rows // 16, across, 0)

        flat = table.reshape(EXAMPLES, chunks * rows, LANES)
        lane = lax.broadcasted_iota(jnp.int32, (LANES, BATCH), 0)

        def sample(n, _):
            base = n * BATCH

            def pick(i, _):
                for u in range(UNROLL):
                    k = i * UNROLL + u
                    place = place_ref[base + k]
                    for e in range(EXAMPLES):
                        picked[e, pl.ds(k, 1), :] = flat[e, pl.ds(place, 1), :]
                return 0

            lax.fori_loop(0, BATCH // UNROLL, pick, 0)
            at = pl.ds(pl.multiple_of(base, BATCH), BATCH)
            keep = lane == low_ref[:, at]
            for e in range(EXAMPLES):
                high, low = split(picked[e])
                dims = (((1,), (1,)), ((), ()))
                values = lax.dot_general(lane_ref[...], high, dims, preferred_element_type=jnp.float32)
                values = values + lax.dot_general(lane_ref[...], low, dims, preferred_element_type=jnp.float32)
                out_ref[e:e + 1, at] = jnp.sum(jnp.where(keep, values, 0.0), axis=0, keepdims=True)
            return 0

        lax.fori_loop(0, samples // BATCH, sample, 0)


def sketch(hidden, grad, ids, sign_bits, place, low):
    rows, tokens = hidden.shape
    columns = grad.shape[1]
    order = min(rows, 256)
    chunks = columns // LANES
    whole = lambda j, place: (0, 0)
    half = sylvester(order)
    return pl.pallas_call(
        functools.partial(kernel, order),
        out_shape=jax.ShapeDtypeStruct((EXAMPLES, low.shape[1]), jnp.float32),
        grid_spec=pltpu.PrefetchScalarGridSpec(
            num_scalar_prefetch=1,
            grid=(columns // WIDE,),
            in_specs=[
                pl.BlockSpec((tokens, LANES), whole),
                pl.BlockSpec((1, low.shape[1]), whole),
                pl.BlockSpec((rows, tokens), whole),
                pl.BlockSpec((tokens, WIDE), lambda j, place: (0, j)),
                pl.BlockSpec((rows, WIDE), lambda j, place: (0, j)),
                pl.BlockSpec((order, 2 * order), whole),
                pl.BlockSpec((LANES, LANES), whole),
            ],
            out_specs=pl.BlockSpec((EXAMPLES, low.shape[1]), whole),
            scratch_shapes=[
                pltpu.VMEM((EXAMPLES, chunks, rows, LANES), jnp.float32),
                pltpu.VMEM((rows // order, order, WIDE), jnp.float32),
                pltpu.VMEM((rows // order, 2 * order, WIDE), jnp.bfloat16),
                pltpu.VMEM((EXAMPLES, BATCH, LANES), jnp.float32),
            ],
        ),
        compiler_params=pltpu.CompilerParams(vmem_limit_bytes=56 << 20),
        name="sketch",
    )(place, ids, low, hidden, grad, sign_bits, jnp.concatenate([half, half], axis=1), sylvester(LANES))


def gather_kernel(
    rows, chips, hidden_ref, ids_ref, grad_ref, hidden_out, ids_out, grad_out,
    own_sem, row_send, row_recv, chip_send, chip_recv, core_send, core_recv,
):
    me = lax.axis_index("row")
    col = lax.axis_index("col")
    chip, core = col // 2, col % 2
    tokens = ids_ref.shape[0]
    high = hidden_ref.shape[0] // PIECES
    count = grad_ref.shape[0]
    deep = count // PIECES

    def row_copy(origin, piece, up):
        at = pl.ds(pl.multiple_of(origin * count + piece * deep, deep), deep)
        return pltpu.make_async_remote_copy(
            src_ref=grad_out.at[at, :], dst_ref=grad_out.at[at, :],
            send_sem=row_send.at[up, origin, piece], recv_sem=row_recv.at[origin, piece],
            device_id={"row": me + 1 if up else me - 1}, device_id_type=MESH,
        )

    def row_first(piece, up):
        at = pl.ds(pl.multiple_of(me * count + piece * deep, deep), deep)
        return pltpu.make_async_remote_copy(
            src_ref=grad_ref.at[pl.ds(piece * deep, deep), :], dst_ref=grad_out.at[at, :],
            send_sem=row_send.at[up, me, piece], recv_sem=row_recv.at[me, piece],
            device_id={"row": me + 1 if up else me - 1}, device_id_type=MESH,
        )

    def hidden_view(origin, piece):
        if piece == PIECES:
            return ids_out.at[pl.ds(pl.multiple_of(origin * tokens, tokens), tokens), :]
        return hidden_out.at[pl.ds(piece * high, high), pl.ds(pl.multiple_of(origin * tokens, tokens), tokens)]

    def hidden_copy(origin, piece, send, recv, target, own):
        view = hidden_view(origin, piece)
        source = view
        if own:
            source = ids_ref if piece == PIECES else hidden_ref.at[pl.ds(piece * high, high), :]
        return pltpu.make_async_remote_copy(
            src_ref=source, dst_ref=view, send_sem=send, recv_sem=recv.at[origin, piece],
            device_id={"col": target}, device_id_type=MESH,
        )

    def chip_copy(origin_chip, piece, up, own=False):
        origin = origin_chip * 2 + core
        return hidden_copy(origin, piece, chip_send.at[up, origin, piece], chip_recv, col + 2 if up else col - 2, own)

    def core_copy(origin, piece, own=False):
        return hidden_copy(origin, piece, core_send.at[origin, piece], core_recv, chip * 2 + 1 - core, own)

    sides = [
        (me > 0, {"row": me - 1}), (me < rows - 1, {"row": me + 1}),
        (chip > 0, {"col": col - 2}), (chip < chips - 1, {"col": col + 2}),
        (core >= 0, {"col": chip * 2 + 1 - core}),
    ]
    barrier = pltpu.get_barrier_semaphore()
    for there, target in sides:
        @pl.when(there)
        def _():
            pl.semaphore_signal(barrier, inc=1, device_id=target, device_id_type=MESH)
    pl.semaphore_wait(barrier, sum(there.astype(jnp.int32) for there, _ in sides))

    kinds = [PIECES] + list(range(PIECES))
    for piece in range(PIECES):
        for up in (0, 1):
            @pl.when(me < rows - 1 if up else me > 0)
            def _():
                row_first(piece, up).start()
    for piece in kinds:
        for up in (0, 1):
            @pl.when(chip < chips - 1 if up else chip > 0)
            def _():
                chip_copy(chip, piece, up, own=True).start()
        core_copy(col, piece, own=True).start()
    mine = [
        pltpu.make_async_copy(hidden_ref, hidden_out.at[:, pl.ds(pl.multiple_of(col * tokens, tokens), tokens)], own_sem.at[0]),
        pltpu.make_async_copy(ids_ref, hidden_view(col, PIECES), own_sem.at[1]),
        pltpu.make_async_copy(grad_ref, grad_out.at[pl.ds(pl.multiple_of(me * count, count), count), :], own_sem.at[2]),
    ]
    for copy in mine:
        copy.start()

    for far in range(1, max(rows, chips)):
        for piece in kinds:
            for up in (0, 1):
                if far < rows and piece < PIECES:
                    origin = me - far if up else me + far

                    @pl.when(origin >= 0 if up else origin < rows)
                    def _():
                        row_copy(origin, piece, up).wait_recv()

                        @pl.when(me < rows - 1 if up else me > 0)
                        def _():
                            row_copy(origin, piece, up).start()
                if far < chips:
                    source = chip - far if up else chip + far

                    @pl.when(source >= 0 if up else source < chips)
                    def _():
                        chip_copy(source, piece, up).wait_recv()

                        @pl.when(chip < chips - 1 if up else chip > 0)
                        def _():
                            chip_copy(source, piece, up).start()
                        core_copy(source * 2 + core, piece).start()

    for copy in mine:
        copy.wait()
    for place in range(chips):
        for piece in kinds:
            core_copy(place * 2 + 1 - core, piece).wait_recv()
            core_copy(place * 2 + core, piece).wait_send()
    for far in range(max(rows, chips)):
        for piece in kinds:
            for up in (0, 1):
                if far < rows and piece < PIECES:
                    origin = me - far if up else me + far

                    @pl.when((origin >= 0) & (me < rows - 1) if up else (origin < rows) & (me > 0))
                    def _():
                        row_copy(origin, piece, up).wait_send()
                if far < chips:
                    source = chip - far if up else chip + far

                    @pl.when((source >= 0) & (chip < chips - 1) if up else (source < chips) & (chip > 0))
                    def _():
                        chip_copy(source, piece, up).wait_send()


def gather(hidden, ids, grad, rows, cols):
    units, tokens = hidden.shape
    shape = jax.ShapeDtypeStruct
    anywhere = pl.BlockSpec(memory_space=pl.ANY)
    dma = pltpu.SemaphoreType.DMA
    return pl.pallas_call(
        functools.partial(gather_kernel, rows, cols // 2),
        out_shape=(
            shape((units, tokens * cols), jnp.bfloat16),
            shape((tokens * cols, LANES), jnp.bfloat16),
            shape((grad.shape[0] * rows, grad.shape[1]), jnp.bfloat16),
        ),
        in_specs=[anywhere] * 3,
        out_specs=[anywhere] * 3,
        scratch_shapes=[
            dma((3,)), dma((2, rows, PIECES)), dma((rows, PIECES)),
            dma((2, cols, PIECES + 1)), dma((cols, PIECES + 1)),
            dma((cols, PIECES + 1)), dma((cols, PIECES + 1)),
        ],
        compiler_params=pltpu.CompilerParams(collective_id=0, has_side_effects=True),
        name="gather",
    )(hidden, ids, grad)


def reduce_kernel(rows, cols, terms_ref, out_ref, arrived, send_sem, recv_sem):
    me = lax.axis_index("row") * cols + lax.axis_index("col")
    count = rows * cols

    def copy(t):
        target = lax.rem(me + t, count)
        return pltpu.make_async_remote_copy(
            src_ref=terms_ref.at[target], dst_ref=arrived.at[me],
            send_sem=send_sem.at[t], recv_sem=recv_sem.at[t],
            device_id={"row": target // cols, "col": lax.rem(target, cols)}, device_id_type=MESH,
        )

    def greet(t, _):
        target = lax.rem(me + t, count)
        pl.semaphore_signal(
            barrier, inc=1, device_id={"row": target // cols, "col": lax.rem(target, cols)}, device_id_type=MESH
        )
        return 0

    barrier = pltpu.get_barrier_semaphore()
    lax.fori_loop(1, count, greet, 0)
    pl.semaphore_wait(barrier, count - 1)
    lax.fori_loop(1, count, lambda t, _: (copy(t).start(), 0)[1], 0)
    arrived[me] = terms_ref[me]
    lax.fori_loop(1, count, lambda t, _: (copy(t).wait(), 0)[1], 0)
    out_ref[...] = jnp.sum(arrived[...], axis=0)


def reduce(terms, rows, cols):
    return pl.pallas_call(
        functools.partial(reduce_kernel, rows, cols),
        out_shape=jax.ShapeDtypeStruct(terms.shape[1:], jnp.float32),
        in_specs=[pl.BlockSpec(memory_space=pltpu.VMEM)],
        out_specs=pl.BlockSpec(memory_space=pltpu.VMEM),
        scratch_shapes=[
            pltpu.VMEM(terms.shape, jnp.float32),
            pltpu.SemaphoreType.DMA((rows * cols,)),
            pltpu.SemaphoreType.DMA((rows * cols,)),
        ],
        compiler_params=pltpu.CompilerParams(collective_id=1, has_side_effects=True),
        name="reduce",
    )(terms)


def shards(hidden, grad_out, example_ids, sign_bits, sample_index):
    row_block = hidden.shape[1]
    col_block = grad_out.shape[1]
    row_count = lax.axis_size("row")
    col_count = lax.axis_size("col")
    d_total = col_block * col_count
    labels = jnp.broadcast_to(example_ids[:, None], (hidden.shape[0], LANES)).astype(jnp.bfloat16)
    hidden_all, ids, grad_all = gather(hidden.T, labels, grad_out, row_count, col_count)
    row_global = sample_index // d_total
    col_global = sample_index % d_total
    row_inner = row_global % row_block
    col_inner = col_global % col_block
    place = (col_inner // LANES) * row_block + row_inner
    low = (col_inner % LANES)[None, :]
    common = jnp.bitwise_count((row_global // row_block) & lax.axis_index("row"))
    common += jnp.bitwise_count((col_global // col_block) & lax.axis_index("col"))
    scale = 1.0 / math.sqrt(row_block * row_count * d_total * TOK_EX)
    weight = jnp.where(common % 2 == 0, scale, -scale).astype(jnp.float32)
    terms = sketch(hidden_all, grad_all, ids, sign_bits, place, low) * weight[None, :]
    terms = terms.reshape(EXAMPLES, row_count * col_count, -1).transpose(1, 0, 2)
    return reduce(terms, row_count, col_count)


def solution(mesh):
    placed = (
        P(("groups", "col"), "row"),
        P(("groups", "row"), "col"),
        P(("groups", "col")),
        P("row", "col"),
        P(),
    )
    return jax.shard_map(
        shards, mesh=mesh, in_specs=placed, out_specs=P("groups", ("row", "col")), check_vma=False
    )
```

```python
import functools
import math

import jax
import jax.numpy as jnp
import numpy as np
from jax import lax
from jax.experimental import pallas as pl
from jax.experimental.pallas import tpu as pltpu
from jax.sharding import PartitionSpec as P

EXAMPLES = 2
TOK_EX = 512
LANES = 128
WIDE = 256
UNROLL = 16
BATCH = 1024
PIECES = 4
GROUP = 4
FUSED = 4
MESH = pl.DeviceIdType.MESH


def sylvester(order):
    table = np.ones((1, 1), np.float32)
    while table.shape[0] < order:
        table = np.block([[table, table], [table, -table]])
    return jnp.asarray(table, jnp.bfloat16)


def butterfly(values):
    span = 1
    values = list(values)
    while span < len(values):
        for start in range(0, len(values), 2 * span):
            for i in range(start, start + span):
                a, b = values[i], values[i + span]
                values[i], values[i + span] = a + b, a - b
        span *= 2
    return values


def split(values):
    high = values.astype(jnp.bfloat16)
    return high, (values - high.astype(jnp.float32)).astype(jnp.bfloat16)


def sample_kernel(place_ref, low_ref, mixed_ref, lane_ref, out_ref, table, picked):
    step = pl.program_id(0)
    chunks, tile = mixed_ref.shape[1:3]
    rows = table.shape[2]
    tiles = rows // tile
    example, start = step // tiles, (step % tiles) * tile
    samples = low_ref.shape[1]

    def across(i, _):
        at = pl.ds(pl.multiple_of(i * 16, 16), 16)
        to = pl.ds(pl.multiple_of(start + i * 16, 16), 16)
        values = butterfly([mixed_ref[0, c, at, :] for c in range(chunks)])
        for c in range(chunks):
            table[example, c, to, :] = values[c]
        return 0

    lax.fori_loop(0, tile // 16, across, 0)

    @pl.when(step == pl.num_programs(0) - 1)
    def _():
        flat = table.reshape(EXAMPLES, chunks * rows, LANES)
        lane = lax.broadcasted_iota(jnp.int32, (LANES, BATCH), 0)

        def sample(n, _):
            base = n * BATCH

            def pick(i, _):
                for u in range(UNROLL):
                    k = i * UNROLL + u
                    place = place_ref[base + k]
                    for e in range(EXAMPLES):
                        picked[e, pl.ds(k, 1), :] = flat[e, pl.ds(place, 1), :]
                return 0

            lax.fori_loop(0, BATCH // UNROLL, pick, 0)
            at = pl.ds(pl.multiple_of(base, BATCH), BATCH)
            keep = lane == low_ref[:, at]
            for e in range(EXAMPLES):
                high, low = split(picked[e])
                dims = (((1,), (1,)), ((), ()))
                values = lax.dot_general(lane_ref[...], high, dims, preferred_element_type=jnp.float32)
                values = values + lax.dot_general(lane_ref[...], low, dims, preferred_element_type=jnp.float32)
                out_ref[e:e + 1, at] = jnp.sum(jnp.where(keep, values, 0.0), axis=0, keepdims=True)
            return 0

        lax.fori_loop(0, samples // BATCH, sample, 0)


def sample(mixed, place, low):
    _, chunks, rows, _ = mixed.shape
    tile = min(rows, 512)
    whole = lambda j, place: (0, 0)
    return pl.pallas_call(
        sample_kernel,
        out_shape=jax.ShapeDtypeStruct((EXAMPLES, low.shape[1]), jnp.float32),
        grid_spec=pltpu.PrefetchScalarGridSpec(
            num_scalar_prefetch=1,
            grid=(EXAMPLES * (rows // tile),),
            in_specs=[
                pl.BlockSpec((1, low.shape[1]), whole),
                pl.BlockSpec((1, chunks, tile, LANES), lambda j, place: (j // (rows // tile), 0, j % (rows // tile), 0)),
                pl.BlockSpec((LANES, LANES), whole),
            ],
            out_specs=pl.BlockSpec((EXAMPLES, low.shape[1]), whole),
            scratch_shapes=[
                pltpu.VMEM((EXAMPLES, chunks, rows, LANES), jnp.float32),
                pltpu.VMEM((EXAMPLES, BATCH, LANES), jnp.float32),
            ],
        ),
        compiler_params=pltpu.CompilerParams(vmem_limit_bytes=56 << 20),
        name="sample",
    )(place, low, mixed, sylvester(LANES))


def gather_kernel(
    rows, chips, order, hidden_ref, ids_ref, grad_ref, sign_ref, pair_ref, mixed_ref,
    hidden_out, ids_out, grad_out, signs, flipped, parts, staged, sign_sem, out_sem, own_sem, row_send, row_recv, chip_send, chip_recv, core_send, core_recv,
):
    me = lax.axis_index("row")
    col = lax.axis_index("col")
    chip, core = col // 2, col % 2
    tokens = ids_ref.shape[0]
    high = hidden_ref.shape[0] // PIECES
    count = grad_ref.shape[0]
    units = hidden_ref.shape[0]
    steps = grad_ref.shape[1] // WIDE
    halves = WIDE // LANES
    blocks = units // order

    def row_copy(origin, piece, up):
        view = grad_out.at[pl.ds(pl.multiple_of(origin * count, count), count), pl.ds(piece * WIDE, WIDE)]
        return pltpu.make_async_remote_copy(
            src_ref=view, dst_ref=view,
            send_sem=row_send.at[up, origin, piece], recv_sem=row_recv.at[origin, piece],
            device_id={"row": me + 1 if up else me - 1}, device_id_type=MESH,
        )

    def row_first(piece, up):
        wide = pl.ds(piece * WIDE, WIDE)
        return pltpu.make_async_remote_copy(
            src_ref=grad_ref.at[:, wide], dst_ref=grad_out.at[pl.ds(pl.multiple_of(me * count, count), count), wide],
            send_sem=row_send.at[up, me, piece], recv_sem=row_recv.at[me, piece],
            device_id={"row": me + 1 if up else me - 1}, device_id_type=MESH,
        )

    def hidden_view(origin, piece):
        if piece == PIECES:
            return ids_out.at[pl.ds(pl.multiple_of(origin * tokens, tokens), tokens), :]
        return hidden_out.at[pl.ds(piece * high, high), pl.ds(pl.multiple_of(origin * tokens, tokens), tokens)]

    def hidden_copy(origin, piece, send, recv, target, own):
        view = hidden_view(origin, piece)
        source = view
        if own:
            source = ids_ref if piece == PIECES else hidden_ref.at[pl.ds(piece * high, high), :]
        return pltpu.make_async_remote_copy(
            src_ref=source, dst_ref=view, send_sem=send, recv_sem=recv.at[origin, piece],
            device_id={"col": target}, device_id_type=MESH,
        )

    def chip_copy(origin_chip, piece, up, own=False):
        origin = origin_chip * 2 + core
        return hidden_copy(origin, piece, chip_send.at[up, origin, piece], chip_recv, col + 2 if up else col - 2, own)

    def core_copy(origin, piece, own=False):
        return hidden_copy(origin, piece, core_send.at[origin, piece], core_recv, chip * 2 + 1 - core, own)

    sides = [
        (me > 0, {"row": me - 1}), (me < rows - 1, {"row": me + 1}),
        (chip > 0, {"col": col - 2}), (chip < chips - 1, {"col": col + 2}),
        (core >= 0, {"col": chip * 2 + 1 - core}),
    ]
    barrier = pltpu.get_barrier_semaphore()
    for there, target in sides:
        @pl.when(there)
        def _():
            pl.semaphore_signal(barrier, inc=1, device_id=target, device_id_type=MESH)
    pl.semaphore_wait(barrier, sum(there.astype(jnp.int32) for there, _ in sides))

    kinds = [PIECES] + list(range(PIECES))
    for piece in range(steps):
        for up in (0, 1):
            @pl.when(me < rows - 1 if up else me > 0)
            def _():
                row_first(piece, up).start()
    for piece in kinds:
        for up in (0, 1):
            @pl.when(chip < chips - 1 if up else chip > 0)
            def _():
                chip_copy(chip, piece, up, own=True).start()
        core_copy(col, piece, own=True).start()
    mine = [
        pltpu.make_async_copy(hidden_ref, hidden_out.at[:, pl.ds(pl.multiple_of(col * tokens, tokens), tokens)], own_sem.at[0]),
        pltpu.make_async_copy(ids_ref, hidden_view(col, PIECES), own_sem.at[1]),
        pltpu.make_async_copy(grad_ref, grad_out.at[pl.ds(pl.multiple_of(me * count, count), count), :], own_sem.at[2]),
    ]
    for copy in mine:
        copy.start()

    def sign_copy(step):
        wide = pl.ds(step * WIDE, WIDE)
        return pltpu.make_async_copy(sign_ref.at[:, wide], signs.at[:, wide], sign_sem.at[step])

    for step in range(steps):
        sign_copy(step).start()

    for far in range(1, max(rows, chips)):
        for piece in kinds:
            for up in (0, 1):
                if far < rows - 1 and piece < steps:
                    origin = me - far if up else me + far

                    @pl.when(origin >= 0 if up else origin < rows)
                    def _():
                        row_copy(origin, piece, up).wait_recv()

                        @pl.when(me < rows - 1 if up else me > 0)
                        def _():
                            row_copy(origin, piece, up).start()
                if far < chips:
                    source = chip - far if up else chip + far

                    @pl.when(source >= 0 if up else source < chips)
                    def _():
                        chip_copy(source, piece, up).wait_recv()

                        @pl.when(chip < chips - 1 if up else chip > 0)
                        def _():
                            chip_copy(source, piece, up).start()
                        core_copy(source * 2 + core, piece).start()

    for copy in mine:
        copy.wait()
    for place in range(chips):
        for piece in kinds:
            core_copy(place * 2 + 1 - core, piece).wait_recv()

    def out_copy(step, e):
        return pltpu.make_async_copy(
            staged.at[step % 2, e], mixed_ref.at[e, pl.ds(step * halves, halves)], out_sem.at[step % 2, e]
        )

    for step in range(steps):
        far = rows - 1
        for up in (0, 1):
            origin = me - far if up else me + far

            @pl.when(origin >= 0 if up else origin < rows)
            def _():
                row_copy(origin, step, up).wait_recv()
        sign_copy(step).wait()
        wide = pl.ds(step * WIDE, WIDE)
        labels = jnp.concatenate([ids_out[...]] * halves, axis=1).astype(jnp.float32)
        for e in range(EXAMPLES):
            masked = jnp.where(labels == e, grad_out[:, wide].astype(jnp.float32), 0.0).astype(jnp.bfloat16)
            group = min(blocks, GROUP)

            def multiply(b, _):
                at = pl.ds(pl.multiple_of(b * group * order, group * order), group * order)
                grads = jnp.dot(hidden_out[at, :], masked, preferred_element_type=jnp.float32)
                flipped[at, :] = jnp.where(signs[at, wide] == 0, grads, -grads)
                return 0

            lax.fori_loop(0, blocks // group, multiply, 0)

            def mix(i, _):
                values = butterfly([
                    flipped[pl.ds(pl.multiple_of(b * order + i * 16, 16), 16), :] for b in range(blocks)
                ])
                at = pl.ds(pl.multiple_of(i * 16, 16), 16)
                below = pl.ds(pl.multiple_of(order + i * 16, 16), 16)
                for b in range(blocks):
                    high, low = split(values[b])
                    parts[b, at, :] = high
                    parts[b, below, :] = low
                return 0

            lax.fori_loop(0, order // 16, mix, 0)
            if step >= 2:
                out_copy(step - 2, e).wait()
            fused = min(blocks, FUSED)

            def transform(i, _):
                for u in range(fused):
                    b = i * fused + u
                    at = pl.ds(pl.multiple_of(b * order, order), order)
                    values = jnp.dot(pair_ref[...], parts[b], preferred_element_type=jnp.float32)
                    for half in range(halves):
                        staged[step % 2, e, half, at, :] = values[:, half * LANES:(half + 1) * LANES]
                return 0

            lax.fori_loop(0, blocks // fused, transform, 0)
            out_copy(step, e).start()
    for step in range(max(0, steps - 2), steps):
        for e in range(EXAMPLES):
            out_copy(step, e).wait()

    for place in range(chips):
        for piece in kinds:
            core_copy(place * 2 + core, piece).wait_send()
    for far in range(max(rows, chips)):
        for piece in kinds:
            for up in (0, 1):
                if far < rows and piece < steps:
                    origin = me - far if up else me + far

                    @pl.when((origin >= 0) & (me < rows - 1) if up else (origin < rows) & (me > 0))
                    def _():
                        row_copy(origin, piece, up).wait_send()
                if far < chips:
                    source = chip - far if up else chip + far

                    @pl.when((source >= 0) & (chip < chips - 1) if up else (source < chips) & (chip > 0))
                    def _():
                        chip_copy(source, piece, up).wait_send()


def mix_rows(hidden, ids, grad, sign_bits, rows, cols):
    units, tokens = hidden.shape
    depth, columns = tokens * cols, grad.shape[1]
    order = min(units, 256)
    half = sylvester(order)
    anywhere = pl.BlockSpec(memory_space=pl.ANY)
    inside = pl.BlockSpec(memory_space=pltpu.VMEM)
    dma = pltpu.SemaphoreType.DMA
    return pl.pallas_call(
        functools.partial(gather_kernel, rows, cols // 2, order),
        out_shape=jax.ShapeDtypeStruct((EXAMPLES, columns // LANES, units, LANES), jnp.float32),
        in_specs=[inside, inside, inside, anywhere, inside],
        out_specs=anywhere,
        scratch_shapes=[
            pltpu.VMEM((units, depth), jnp.bfloat16),
            pltpu.VMEM((depth, LANES), jnp.bfloat16),
            pltpu.VMEM((depth, columns), jnp.bfloat16),
            pltpu.VMEM((units, columns), jnp.int32),
            pltpu.VMEM((units, WIDE), jnp.float32),
            pltpu.VMEM((units // order, 2 * order, WIDE), jnp.bfloat16),
            pltpu.VMEM((2, EXAMPLES, WIDE // LANES, units, LANES), jnp.float32),
            dma((columns // WIDE,)), dma((2, EXAMPLES)),
            dma((3,)), dma((2, rows, columns // WIDE)), dma((rows, columns // WIDE)),
            dma((2, cols, PIECES + 1)), dma((cols, PIECES + 1)),
            dma((cols, PIECES + 1)), dma((cols, PIECES + 1)),
        ],
        compiler_params=pltpu.CompilerParams(collective_id=0, has_side_effects=True, vmem_limit_bytes=56 << 20),
        name="mix_rows",
    )(hidden, ids, grad, sign_bits, jnp.concatenate([half, half], axis=1))


def reduce_kernel(rows, cols, terms_ref, out_ref, arrived, send_sem, recv_sem):
    me = lax.axis_index("row") * cols + lax.axis_index("col")
    count = rows * cols

    def copy(t):
        target = lax.rem(me + t, count)
        return pltpu.make_async_remote_copy(
            src_ref=terms_ref.at[target], dst_ref=arrived.at[me],
            send_sem=send_sem.at[t], recv_sem=recv_sem.at[t],
            device_id={"row": target // cols, "col": lax.rem(target, cols)}, device_id_type=MESH,
        )

    def greet(t, _):
        target = lax.rem(me + t, count)
        pl.semaphore_signal(
            barrier, inc=1, device_id={"row": target // cols, "col": lax.rem(target, cols)}, device_id_type=MESH
        )
        return 0

    barrier = pltpu.get_barrier_semaphore()
    lax.fori_loop(1, count, greet, 0)
    pl.semaphore_wait(barrier, count - 1)
    lax.fori_loop(1, count, lambda t, _: (copy(t).start(), 0)[1], 0)
    arrived[me] = terms_ref[me]
    lax.fori_loop(1, count, lambda t, _: (copy(t).wait(), 0)[1], 0)
    out_ref[...] = jnp.sum(arrived[...], axis=0)


def reduce(terms, rows, cols):
    return pl.pallas_call(
        functools.partial(reduce_kernel, rows, cols),
        out_shape=jax.ShapeDtypeStruct(terms.shape[1:], jnp.float32),
        in_specs=[pl.BlockSpec(memory_space=pltpu.VMEM)],
        out_specs=pl.BlockSpec(memory_space=pltpu.VMEM),
        scratch_shapes=[
            pltpu.VMEM(terms.shape, jnp.float32),
            pltpu.SemaphoreType.DMA((rows * cols,)),
            pltpu.SemaphoreType.DMA((rows * cols,)),
        ],
        compiler_params=pltpu.CompilerParams(collective_id=1, has_side_effects=True),
        name="reduce",
    )(terms)


def shards(hidden, grad_out, example_ids, sign_bits, sample_index):
    row_block = hidden.shape[1]
    col_block = grad_out.shape[1]
    row_count = lax.axis_size("row")
    col_count = lax.axis_size("col")
    d_total = col_block * col_count
    labels = jnp.broadcast_to(example_ids[:, None], (hidden.shape[0], LANES)).astype(jnp.bfloat16)
    mixed = mix_rows(hidden.T, labels, grad_out, sign_bits, row_count, col_count)
    row_global = sample_index // d_total
    col_global = sample_index % d_total
    row_inner = row_global % row_block
    col_inner = col_global % col_block
    place = (col_inner // LANES) * row_block + row_inner
    low = (col_inner % LANES)[None, :]
    common = jnp.bitwise_count((row_global // row_block) & lax.axis_index("row"))
    common += jnp.bitwise_count((col_global // col_block) & lax.axis_index("col"))
    scale = 1.0 / math.sqrt(row_block * row_count * d_total * TOK_EX)
    weight = jnp.where(common % 2 == 0, scale, -scale).astype(jnp.float32)
    terms = sample(mixed, place, low) * weight[None, :]
    terms = terms.reshape(EXAMPLES, row_count * col_count, -1).transpose(1, 0, 2)
    return reduce(terms, row_count, col_count)


def solution(mesh):
    placed = (
        P(("groups", "col"), "row"),
        P(("groups", "row"), "col"),
        P(("groups", "col")),
        P("row", "col"),
        P(),
    )
    return jax.shard_map(
        shards, mesh=mesh, in_specs=placed, out_specs=P("groups", ("row", "col")), check_vma=False
    )
```

```python
import functools
import math

import jax
import jax.numpy as jnp
import numpy as np
from jax import lax
from jax.experimental import pallas as pl
from jax.experimental.pallas import tpu as pltpu
from jax.sharding import PartitionSpec as P

EXAMPLES = 2
TOK_EX = 512
LANES = 128
WIDE = 256
UNROLL = 16
BATCH = 1024
PIECES = 4
GROUP = 8
FUSED = 8
MESH = pl.DeviceIdType.MESH


def sylvester(order):
    table = np.ones((1, 1), np.float32)
    while table.shape[0] < order:
        table = np.block([[table, table], [table, -table]])
    return jnp.asarray(table, jnp.bfloat16)


def butterfly(values):
    span = 1
    values = list(values)
    while span < len(values):
        for start in range(0, len(values), 2 * span):
            for i in range(start, start + span):
                a, b = values[i], values[i + span]
                values[i], values[i + span] = a + b, a - b
        span *= 2
    return values


def split(values):
    high = values.astype(jnp.bfloat16)
    return high, (values - high.astype(jnp.float32)).astype(jnp.bfloat16)


def sample_kernel(place_ref, low_ref, mixed_ref, lane_ref, out_ref, table, picked):
    step = pl.program_id(0)
    chunks, tile = mixed_ref.shape[1:3]
    rows = table.shape[2]
    tiles = rows // tile
    example, start = step // tiles, (step % tiles) * tile
    samples = low_ref.shape[1]

    def across(i, _):
        at = pl.ds(pl.multiple_of(i * 16, 16), 16)
        to = pl.ds(pl.multiple_of(start + i * 16, 16), 16)
        values = butterfly([mixed_ref[0, c, at, :] for c in range(chunks)])
        for c in range(chunks):
            table[example, c, to, :] = values[c]
        return 0

    lax.fori_loop(0, tile // 16, across, 0)

    @pl.when(step == pl.num_programs(0) - 1)
    def _():
        flat = table.reshape(EXAMPLES, chunks * rows, LANES)
        lane = lax.broadcasted_iota(jnp.int32, (LANES, BATCH), 0)

        def sample(n, _):
            base = n * BATCH

            def pick(i, _):
                for u in range(UNROLL):
                    k = i * UNROLL + u
                    place = place_ref[base + k]
                    for e in range(EXAMPLES):
                        picked[e, pl.ds(k, 1), :] = flat[e, pl.ds(place, 1), :]
                return 0

            lax.fori_loop(0, BATCH // UNROLL, pick, 0)
            at = pl.ds(pl.multiple_of(base, BATCH), BATCH)
            keep = lane == low_ref[:, at]
            for e in range(EXAMPLES):
                high, low = split(picked[e])
                dims = (((1,), (1,)), ((), ()))
                values = lax.dot_general(lane_ref[...], high, dims, preferred_element_type=jnp.float32)
                values = values + lax.dot_general(lane_ref[...], low, dims, preferred_element_type=jnp.float32)
                out_ref[e:e + 1, at] = jnp.sum(jnp.where(keep, values, 0.0), axis=0, keepdims=True)
            return 0

        lax.fori_loop(0, samples // BATCH, sample, 0)


def sample(mixed, place, low):
    _, chunks, rows, _ = mixed.shape
    tile = min(rows, 512)
    whole = lambda j, place: (0, 0)
    return pl.pallas_call(
        sample_kernel,
        out_shape=jax.ShapeDtypeStruct((EXAMPLES, low.shape[1]), jnp.float32),
        grid_spec=pltpu.PrefetchScalarGridSpec(
            num_scalar_prefetch=1,
            grid=(EXAMPLES * (rows // tile),),
            in_specs=[
                pl.BlockSpec((1, low.shape[1]), whole),
                pl.BlockSpec((1, chunks, tile, LANES), lambda j, place: (j // (rows // tile), 0, j % (rows // tile), 0)),
                pl.BlockSpec((LANES, LANES), whole),
            ],
            out_specs=pl.BlockSpec((EXAMPLES, low.shape[1]), whole),
            scratch_shapes=[
                pltpu.VMEM((EXAMPLES, chunks, rows, LANES), jnp.float32),
                pltpu.VMEM((EXAMPLES, BATCH, LANES), jnp.float32),
            ],
        ),
        compiler_params=pltpu.CompilerParams(vmem_limit_bytes=56 << 20),
        name="sample",
    )(place, low, mixed, sylvester(LANES))


def gather_kernel(
    rows, chips, order, given_ref, labels_ref, grad_ref, sign_ref, pair_ref, mixed_ref,
    hidden_ref, ids_ref, hidden_out, ids_out, grad_out, signs, flipped, parts, staged, sign_sem, out_sem, own_sem, row_send, row_recv, chip_send, chip_recv, core_send, core_recv,
):
    me = lax.axis_index("row")
    col = lax.axis_index("col")
    chip, core = col // 2, col % 2
    tokens = ids_ref.shape[0]
    high = hidden_ref.shape[0] // PIECES
    count = grad_ref.shape[0]
    units = hidden_ref.shape[0]
    steps = grad_ref.shape[1] // WIDE
    halves = WIDE // LANES
    blocks = units // order

    def row_copy(origin, piece, up):
        view = grad_out.at[pl.ds(pl.multiple_of(origin * count, count), count), pl.ds(piece * WIDE, WIDE)]
        return pltpu.make_async_remote_copy(
            src_ref=view, dst_ref=view,
            send_sem=row_send.at[up, origin, piece], recv_sem=row_recv.at[origin, piece],
            device_id={"row": me + 1 if up else me - 1}, device_id_type=MESH,
        )

    def row_first(piece, up):
        wide = pl.ds(piece * WIDE, WIDE)
        return pltpu.make_async_remote_copy(
            src_ref=grad_ref.at[:, wide], dst_ref=grad_out.at[pl.ds(pl.multiple_of(me * count, count), count), wide],
            send_sem=row_send.at[up, me, piece], recv_sem=row_recv.at[me, piece],
            device_id={"row": me + 1 if up else me - 1}, device_id_type=MESH,
        )

    def hidden_view(origin, piece):
        if piece == PIECES:
            return ids_out.at[pl.ds(pl.multiple_of(origin * tokens, tokens), tokens), :]
        return hidden_out.at[pl.ds(piece * high, high), pl.ds(pl.multiple_of(origin * tokens, tokens), tokens)]

    def hidden_copy(origin, piece, send, recv, target, own):
        view = hidden_view(origin, piece)
        source = view
        if own:
            source = ids_ref if piece == PIECES else hidden_ref.at[pl.ds(piece * high, high), :]
        return pltpu.make_async_remote_copy(
            src_ref=source, dst_ref=view, send_sem=send, recv_sem=recv.at[origin, piece],
            device_id={"col": target}, device_id_type=MESH,
        )

    def chip_copy(origin_chip, piece, up, own=False):
        origin = origin_chip * 2 + core
        return hidden_copy(origin, piece, chip_send.at[up, origin, piece], chip_recv, col + 2 if up else col - 2, own)

    def core_copy(origin, piece, own=False):
        return hidden_copy(origin, piece, core_send.at[origin, piece], core_recv, chip * 2 + 1 - core, own)

    sides = [
        (me > 0, {"row": me - 1}), (me < rows - 1, {"row": me + 1}),
        (chip > 0, {"col": col - 2}), (chip < chips - 1, {"col": col + 2}),
        (core >= 0, {"col": chip * 2 + 1 - core}),
    ]
    barrier = pltpu.get_barrier_semaphore()
    for there, target in sides:
        @pl.when(there)
        def _():
            pl.semaphore_signal(barrier, inc=1, device_id=target, device_id_type=MESH)
    pl.semaphore_wait(barrier, sum(there.astype(jnp.int32) for there, _ in sides))

    kinds = [PIECES] + list(range(PIECES))
    for piece in range(steps):
        for up in (0, 1):
            @pl.when(me < rows - 1 if up else me > 0)
            def _():
                row_first(piece, up).start()
    ids_ref[...] = jnp.broadcast_to(labels_ref[...].astype(jnp.float32), (LANES, tokens)).T.astype(jnp.bfloat16)
    for piece in kinds:
        if piece < PIECES:
            part = given_ref[:, piece * high:(piece + 1) * high].astype(jnp.float32)
            hidden_ref[piece * high:(piece + 1) * high, :] = part.T.astype(jnp.bfloat16)
        for up in (0, 1):
            @pl.when(chip < chips - 1 if up else chip > 0)
            def _():
                chip_copy(chip, piece, up, own=True).start()
        core_copy(col, piece, own=True).start()
    mine = [
        pltpu.make_async_copy(hidden_ref, hidden_out.at[:, pl.ds(pl.multiple_of(col * tokens, tokens), tokens)], own_sem.at[0]),
        pltpu.make_async_copy(ids_ref, hidden_view(col, PIECES), own_sem.at[1]),
        pltpu.make_async_copy(grad_ref, grad_out.at[pl.ds(pl.multiple_of(me * count, count), count), :], own_sem.at[2]),
    ]
    for copy in mine:
        copy.start()

    def sign_copy(step):
        wide = pl.ds(step * WIDE, WIDE)
        return pltpu.make_async_copy(sign_ref.at[:, wide], signs.at[:, wide], sign_sem.at[step])

    for step in range(steps):
        sign_copy(step).start()

    for far in range(1, max(rows, chips)):
        for piece in kinds:
            for up in (0, 1):
                if far < rows - 1 and piece < steps:
                    origin = me - far if up else me + far

                    @pl.when(origin >= 0 if up else origin < rows)
                    def _():
                        row_copy(origin, piece, up).wait_recv()

                        @pl.when(me < rows - 1 if up else me > 0)
                        def _():
                            row_copy(origin, piece, up).start()
                if far < chips:
                    source = chip - far if up else chip + far

                    @pl.when(source >= 0 if up else source < chips)
                    def _():
                        chip_copy(source, piece, up).wait_recv()

                        @pl.when(chip < chips - 1 if up else chip > 0)
                        def _():
                            chip_copy(source, piece, up).start()
                        core_copy(source * 2 + core, piece).start()

    for copy in mine:
        copy.wait()
    for place in range(chips):
        for piece in kinds:
            core_copy(place * 2 + 1 - core, piece).wait_recv()

    def out_copy(step, e):
        return pltpu.make_async_copy(
            staged.at[step % 2, e], mixed_ref.at[e, pl.ds(step * halves, halves)], out_sem.at[step % 2, e]
        )

    for step in range(steps):
        far = rows - 1
        for up in (0, 1):
            origin = me - far if up else me + far

            @pl.when(origin >= 0 if up else origin < rows)
            def _():
                row_copy(origin, step, up).wait_recv()
        sign_copy(step).wait()
        wide = pl.ds(step * WIDE, WIDE)
        labels = jnp.concatenate([ids_out[...]] * halves, axis=1).astype(jnp.float32)
        for e in range(EXAMPLES):
            masked = jnp.where(labels == e, grad_out[:, wide].astype(jnp.float32), 0.0).astype(jnp.bfloat16)
            group = min(blocks, GROUP)

            def multiply(b, _):
                at = pl.ds(pl.multiple_of(b * group * order, group * order), group * order)
                grads = jnp.dot(hidden_out[at, :], masked, preferred_element_type=jnp.float32)
                flipped[at, :] = jnp.where(signs[at, wide] == 0, grads, -grads)
                return 0

            lax.fori_loop(0, blocks // group, multiply, 0)

            def mix(i, _):
                values = butterfly([
                    flipped[pl.ds(pl.multiple_of(b * order + i * 16, 16), 16), :] for b in range(blocks)
                ])
                at = pl.ds(pl.multiple_of(i * 16, 16), 16)
                below = pl.ds(pl.multiple_of(order + i * 16, 16), 16)
                for b in range(blocks):
                    high, low = split(values[b])
                    parts[b, at, :] = high
                    parts[b, below, :] = low
                return 0

            lax.fori_loop(0, order // 16, mix, 0)
            if step >= 2:
                out_copy(step - 2, e).wait()
            fused = min(blocks, FUSED)

            def transform(i, _):
                for u in range(fused):
                    b = i * fused + u
                    at = pl.ds(pl.multiple_of(b * order, order), order)
                    values = jnp.dot(pair_ref[...], parts[b], preferred_element_type=jnp.float32)
                    for half in range(halves):
                        staged[step % 2, e, half, at, :] = values[:, half * LANES:(half + 1) * LANES]
                return 0

            lax.fori_loop(0, blocks // fused, transform, 0)
            out_copy(step, e).start()
    for step in range(max(0, steps - 2), steps):
        for e in range(EXAMPLES):
            out_copy(step, e).wait()

    for place in range(chips):
        for piece in kinds:
            core_copy(place * 2 + core, piece).wait_send()
    for far in range(max(rows, chips)):
        for piece in kinds:
            for up in (0, 1):
                if far < rows and piece < steps:
                    origin = me - far if up else me + far

                    @pl.when((origin >= 0) & (me < rows - 1) if up else (origin < rows) & (me > 0))
                    def _():
                        row_copy(origin, piece, up).wait_send()
                if far < chips:
                    source = chip - far if up else chip + far

                    @pl.when((source >= 0) & (chip < chips - 1) if up else (source < chips) & (chip > 0))
                    def _():
                        chip_copy(source, piece, up).wait_send()


def mix_rows(hidden, ids, grad, sign_bits, rows, cols):
    tokens, units = hidden.shape
    depth, columns = tokens * cols, grad.shape[1]
    order = min(units, 256)
    half = sylvester(order)
    anywhere = pl.BlockSpec(memory_space=pl.ANY)
    inside = pl.BlockSpec(memory_space=pltpu.VMEM)
    dma = pltpu.SemaphoreType.DMA
    return pl.pallas_call(
        functools.partial(gather_kernel, rows, cols // 2, order),
        out_shape=jax.ShapeDtypeStruct((EXAMPLES, columns // LANES, units, LANES), jnp.float32),
        in_specs=[inside, inside, inside, anywhere, inside],
        out_specs=anywhere,
        scratch_shapes=[
            pltpu.VMEM((units, tokens), jnp.bfloat16),
            pltpu.VMEM((tokens, LANES), jnp.bfloat16),
            pltpu.VMEM((units, depth), jnp.bfloat16),
            pltpu.VMEM((depth, LANES), jnp.bfloat16),
            pltpu.VMEM((depth, columns), jnp.bfloat16),
            pltpu.VMEM((units, columns), jnp.int32),
            pltpu.VMEM((units, WIDE), jnp.float32),
            pltpu.VMEM((units // order, 2 * order, WIDE), jnp.bfloat16),
            pltpu.VMEM((2, EXAMPLES, WIDE // LANES, units, LANES), jnp.float32),
            dma((columns // WIDE,)), dma((2, EXAMPLES)),
            dma((3,)), dma((2, rows, columns // WIDE)), dma((rows, columns // WIDE)),
            dma((2, cols, PIECES + 1)), dma((cols, PIECES + 1)),
            dma((cols, PIECES + 1)), dma((cols, PIECES + 1)),
        ],
        compiler_params=pltpu.CompilerParams(collective_id=0, has_side_effects=True, vmem_limit_bytes=56 << 20),
        name="mix_rows",
    )(hidden, ids, grad, sign_bits, jnp.concatenate([half, half], axis=1))


def reduce_kernel(rows, cols, terms_ref, out_ref, arrived, send_sem, recv_sem):
    me = lax.axis_index("row") * cols + lax.axis_index("col")
    count = rows * cols

    def copy(t):
        target = lax.rem(me + t, count)
        return pltpu.make_async_remote_copy(
            src_ref=terms_ref.at[target], dst_ref=arrived.at[me],
            send_sem=send_sem.at[t], recv_sem=recv_sem.at[t],
            device_id={"row": target // cols, "col": lax.rem(target, cols)}, device_id_type=MESH,
        )

    def greet(t, _):
        target = lax.rem(me + t, count)
        pl.semaphore_signal(
            barrier, inc=1, device_id={"row": target // cols, "col": lax.rem(target, cols)}, device_id_type=MESH
        )
        return 0

    barrier = pltpu.get_barrier_semaphore()
    lax.fori_loop(1, count, greet, 0)
    pl.semaphore_wait(barrier, count - 1)
    lax.fori_loop(1, count, lambda t, _: (copy(t).start(), 0)[1], 0)
    arrived[me] = terms_ref[me]
    lax.fori_loop(1, count, lambda t, _: (copy(t).wait(), 0)[1], 0)
    out_ref[...] = jnp.sum(arrived[...], axis=0)


def reduce(terms, rows, cols):
    return pl.pallas_call(
        functools.partial(reduce_kernel, rows, cols),
        out_shape=jax.ShapeDtypeStruct(terms.shape[1:], jnp.float32),
        in_specs=[pl.BlockSpec(memory_space=pltpu.VMEM)],
        out_specs=pl.BlockSpec(memory_space=pltpu.VMEM),
        scratch_shapes=[
            pltpu.VMEM(terms.shape, jnp.float32),
            pltpu.SemaphoreType.DMA((rows * cols,)),
            pltpu.SemaphoreType.DMA((rows * cols,)),
        ],
        compiler_params=pltpu.CompilerParams(collective_id=1, has_side_effects=True),
        name="reduce",
    )(terms)


def shards(hidden, grad_out, example_ids, sign_bits, sample_index):
    row_block = hidden.shape[1]
    col_block = grad_out.shape[1]
    row_count = lax.axis_size("row")
    col_count = lax.axis_size("col")
    d_total = col_block * col_count
    mixed = mix_rows(hidden, example_ids[None, :], grad_out, sign_bits, row_count, col_count)
    row_global = sample_index // d_total
    col_global = sample_index % d_total
    row_inner = row_global % row_block
    col_inner = col_global % col_block
    place = (col_inner // LANES) * row_block + row_inner
    low = (col_inner % LANES)[None, :]
    common = jnp.bitwise_count((row_global // row_block) & lax.axis_index("row"))
    common += jnp.bitwise_count((col_global // col_block) & lax.axis_index("col"))
    scale = 1.0 / math.sqrt(row_block * row_count * d_total * TOK_EX)
    weight = jnp.where(common % 2 == 0, scale, -scale).astype(jnp.float32)
    terms = sample(mixed, place, low) * weight[None, :]
    terms = terms.reshape(EXAMPLES, row_count * col_count, -1).transpose(1, 0, 2)
    return reduce(terms, row_count, col_count)


def solution(mesh):
    placed = (
        P(("groups", "col"), "row"),
        P(("groups", "row"), "col"),
        P(("groups", "col")),
        P("row", "col"),
        P(),
    )
    return jax.shard_map(
        shards, mesh=mesh, in_specs=placed, out_specs=P("groups", ("row", "col")), check_vma=False
    )
```

```python
import functools
import math

import jax
import jax.numpy as jnp
import numpy as np
from jax import lax
from jax.experimental import pallas as pl
from jax.experimental.pallas import tpu as pltpu
from jax.sharding import PartitionSpec as P

EXAMPLES = 2
TOK_EX = 512
LANES = 128
WIDE = 256
UNROLL = 16
BATCH = 1024
PIECES = 4
GROUP = 8
FUSED = 4
MESH = pl.DeviceIdType.MESH


def sylvester(order):
    table = np.ones((1, 1), np.float32)
    while table.shape[0] < order:
        table = np.block([[table, table], [table, -table]])
    return jnp.asarray(table, jnp.bfloat16)


def butterfly(values):
    span = 1
    values = list(values)
    while span < len(values):
        for start in range(0, len(values), 2 * span):
            for i in range(start, start + span):
                a, b = values[i], values[i + span]
                values[i], values[i + span] = a + b, a - b
        span *= 2
    return values


def split(values):
    high = values.astype(jnp.bfloat16)
    return high, (values - high.astype(jnp.float32)).astype(jnp.bfloat16)


def sample_kernel(place_ref, low_ref, mixed_ref, lane_ref, out_ref, table, picked):
    step = pl.program_id(0)
    chunks, tile = mixed_ref.shape[1:3]
    rows = table.shape[2]
    tiles = rows // tile
    example, start = step // tiles, (step % tiles) * tile
    samples = low_ref.shape[1]

    def across(i, _):
        at = pl.ds(pl.multiple_of(i * 16, 16), 16)
        to = pl.ds(pl.multiple_of(start + i * 16, 16), 16)
        values = butterfly([mixed_ref[0, c, at, :] for c in range(chunks)])
        for c in range(chunks):
            table[example, c, to, :] = values[c]
        return 0

    lax.fori_loop(0, tile // 16, across, 0)

    @pl.when(step == pl.num_programs(0) - 1)
    def _():
        flat = table.reshape(EXAMPLES, chunks * rows, LANES)
        lane = lax.broadcasted_iota(jnp.int32, (LANES, BATCH), 0)

        def sample(n, _):
            base = n * BATCH

            def pick(i, _):
                for u in range(UNROLL):
                    k = i * UNROLL + u
                    place = place_ref[base + k]
                    for e in range(EXAMPLES):
                        picked[e, pl.ds(k, 1), :] = flat[e, pl.ds(place, 1), :]
                return 0

            lax.fori_loop(0, BATCH // UNROLL, pick, 0)
            at = pl.ds(pl.multiple_of(base, BATCH), BATCH)
            keep = lane == low_ref[:, at]
            for e in range(EXAMPLES):
                high, low = split(picked[e])
                dims = (((1,), (1,)), ((), ()))
                values = lax.dot_general(lane_ref[...], high, dims, preferred_element_type=jnp.float32)
                values = values + lax.dot_general(lane_ref[...], low, dims, preferred_element_type=jnp.float32)
                out_ref[e:e + 1, at] = jnp.sum(jnp.where(keep, values, 0.0), axis=0, keepdims=True)
            return 0

        lax.fori_loop(0, samples // BATCH, sample, 0)


def sample(mixed, place, low):
    _, chunks, rows, _ = mixed.shape
    tile = min(rows, 512)
    whole = lambda j, place: (0, 0)
    return pl.pallas_call(
        sample_kernel,
        out_shape=jax.ShapeDtypeStruct((EXAMPLES, low.shape[1]), jnp.float32),
        grid_spec=pltpu.PrefetchScalarGridSpec(
            num_scalar_prefetch=1,
            grid=(EXAMPLES * (rows // tile),),
            in_specs=[
                pl.BlockSpec((1, low.shape[1]), whole),
                pl.BlockSpec((1, chunks, tile, LANES), lambda j, place: (j // (rows // tile), 0, j % (rows // tile), 0)),
                pl.BlockSpec((LANES, LANES), whole),
            ],
            out_specs=pl.BlockSpec((EXAMPLES, low.shape[1]), whole),
            scratch_shapes=[
                pltpu.VMEM((EXAMPLES, chunks, rows, LANES), jnp.float32),
                pltpu.VMEM((EXAMPLES, BATCH, LANES), jnp.float32),
            ],
        ),
        compiler_params=pltpu.CompilerParams(vmem_limit_bytes=56 << 20),
        name="sample",
    )(place, low, mixed, sylvester(LANES))


def gather_kernel(
    rows, chips, order, hidden_ref, ids_ref, grad_ref, sign_ref, pair_ref, mixed_ref,
    hidden_out, ids_out, grad_out, signs, flipped, parts, staged, sign_sem, out_sem, own_sem, row_send, row_recv, chip_send, chip_recv, core_send, core_recv,
):
    me = lax.axis_index("row")
    col = lax.axis_index("col")
    chip, core = col // 2, col % 2
    tokens = ids_ref.shape[0]
    high = hidden_ref.shape[0] // PIECES
    count = grad_ref.shape[0]
    units = hidden_ref.shape[0]
    steps = grad_ref.shape[1] // WIDE
    halves = WIDE // LANES
    blocks = units // order

    def row_copy(origin, piece, up):
        view = grad_out.at[pl.ds(pl.multiple_of(origin * count, count), count), pl.ds(piece * WIDE, WIDE)]
        return pltpu.make_async_remote_copy(
            src_ref=view, dst_ref=view,
            send_sem=row_send.at[up, origin, piece], recv_sem=row_recv.at[origin, piece],
            device_id={"row": me + 1 if up else me - 1}, device_id_type=MESH,
        )

    def row_first(piece, up):
        wide = pl.ds(piece * WIDE, WIDE)
        return pltpu.make_async_remote_copy(
            src_ref=grad_ref.at[:, wide], dst_ref=grad_out.at[pl.ds(pl.multiple_of(me * count, count), count), wide],
            send_sem=row_send.at[up, me, piece], recv_sem=row_recv.at[me, piece],
            device_id={"row": me + 1 if up else me - 1}, device_id_type=MESH,
        )

    def hidden_view(origin, piece):
        if piece == PIECES:
            return ids_out.at[pl.ds(pl.multiple_of(origin * tokens, tokens), tokens), :]
        return hidden_out.at[pl.ds(piece * high, high), pl.ds(pl.multiple_of(origin * tokens, tokens), tokens)]

    def hidden_copy(origin, piece, send, recv, target, own):
        view = hidden_view(origin, piece)
        source = view
        if own:
            source = ids_ref if piece == PIECES else hidden_ref.at[pl.ds(piece * high, high), :]
        return pltpu.make_async_remote_copy(
            src_ref=source, dst_ref=view, send_sem=send, recv_sem=recv.at[origin, piece],
            device_id={"col": target}, device_id_type=MESH,
        )

    def chip_copy(origin_chip, piece, up, own=False):
        origin = origin_chip * 2 + core
        return hidden_copy(origin, piece, chip_send.at[up, origin, piece], chip_recv, col + 2 if up else col - 2, own)

    def core_copy(origin, piece, own=False):
        return hidden_copy(origin, piece, core_send.at[origin, piece], core_recv, chip * 2 + 1 - core, own)

    sides = [
        (me > 0, {"row": me - 1}), (me < rows - 1, {"row": me + 1}),
        (chip > 0, {"col": col - 2}), (chip < chips - 1, {"col": col + 2}),
        (core >= 0, {"col": chip * 2 + 1 - core}),
    ]
    barrier = pltpu.get_barrier_semaphore()
    for there, target in sides:
        @pl.when(there)
        def _():
            pl.semaphore_signal(barrier, inc=1, device_id=target, device_id_type=MESH)
    pl.semaphore_wait(barrier, sum(there.astype(jnp.int32) for there, _ in sides))

    kinds = [PIECES] + list(range(PIECES))
    for piece in kinds:
        for up in (0, 1):
            @pl.when(chip < chips - 1 if up else chip > 0)
            def _():
                chip_copy(chip, piece, up, own=True).start()
    for piece in range(steps):
        for up in (0, 1):
            @pl.when(me < rows - 1 if up else me > 0)
            def _():
                row_first(piece, up).start()
    for piece in kinds:
        core_copy(col, piece, own=True).start()
    mine = [
        pltpu.make_async_copy(hidden_ref, hidden_out.at[:, pl.ds(pl.multiple_of(col * tokens, tokens), tokens)], own_sem.at[0]),
        pltpu.make_async_copy(ids_ref, hidden_view(col, PIECES), own_sem.at[1]),
        pltpu.make_async_copy(grad_ref, grad_out.at[pl.ds(pl.multiple_of(me * count, count), count), :], own_sem.at[2]),
    ]
    for copy in mine:
        copy.start()

    def sign_copy(step):
        wide = pl.ds(step * WIDE, WIDE)
        return pltpu.make_async_copy(sign_ref.at[:, wide], signs.at[:, wide], sign_sem.at[step])

    for step in range(steps):
        sign_copy(step).start()

    for far in range(1, max(rows, chips)):
        for piece in kinds:
            for up in (0, 1):
                if far < rows - 1 and piece < steps:
                    origin = me - far if up else me + far

                    @pl.when(origin >= 0 if up else origin < rows)
                    def _():
                        row_copy(origin, piece, up).wait_recv()

                        @pl.when(me < rows - 1 if up else me > 0)
                        def _():
                            row_copy(origin, piece, up).start()
                if far < chips:
                    source = chip - far if up else chip + far

                    @pl.when(source >= 0 if up else source < chips)
                    def _():
                        chip_copy(source, piece, up).wait_recv()

                        @pl.when(chip < chips - 1 if up else chip > 0)
                        def _():
                            chip_copy(source, piece, up).start()
                        core_copy(source * 2 + core, piece).start()

    for copy in mine:
        copy.wait()
    for place in range(chips):
        for piece in kinds:
            core_copy(place * 2 + 1 - core, piece).wait_recv()

    def out_copy(step, e):
        return pltpu.make_async_copy(
            staged.at[step % 2, e], mixed_ref.at[e, pl.ds(step * halves, halves)], out_sem.at[step % 2, e]
        )

    for step in range(steps):
        far = rows - 1
        for up in (0, 1):
            origin = me - far if up else me + far

            @pl.when(origin >= 0 if up else origin < rows)
            def _():
                row_copy(origin, step, up).wait_recv()
        sign_copy(step).wait()
        wide = pl.ds(step * WIDE, WIDE)
        labels = jnp.concatenate([ids_out[...]] * halves, axis=1).astype(jnp.float32)
        for e in range(EXAMPLES):
            masked = jnp.where(labels == e, grad_out[:, wide].astype(jnp.float32), 0.0).astype(jnp.bfloat16)
            group = min(blocks, GROUP)

            def multiply(b, _):
                at = pl.ds(pl.multiple_of(b * group * order, group * order), group * order)
                grads = jnp.dot(hidden_out[at, :], masked, preferred_element_type=jnp.float32)
                flipped[at, :] = jnp.where(signs[at, wide] == 0, grads, -grads)
                return 0

            lax.fori_loop(0, blocks // group, multiply, 0)

            def mix(i, _):
                values = butterfly([
                    flipped[pl.ds(pl.multiple_of(b * order + i * 16, 16), 16), :] for b in range(blocks)
                ])
                at = pl.ds(pl.multiple_of(i * 16, 16), 16)
                below = pl.ds(pl.multiple_of(order + i * 16, 16), 16)
                for b in range(blocks):
                    high, low = split(values[b])
                    parts[b, at, :] = high
                    parts[b, below, :] = low
                return 0

            lax.fori_loop(0, order // 16, mix, 0)
            if step >= 2:
                out_copy(step - 2, e).wait()
            fused = min(blocks, FUSED)

            def transform(i, _):
                for u in range(fused):
                    b = i * fused + u
                    at = pl.ds(pl.multiple_of(b * order, order), order)
                    values = jnp.dot(pair_ref[...], parts[b], preferred_element_type=jnp.float32)
                    for half in range(halves):
                        staged[step % 2, e, half, at, :] = values[:, half * LANES:(half + 1) * LANES]
                return 0

            lax.fori_loop(0, blocks // fused, transform, 0)
            out_copy(step, e).start()
    for step in range(max(0, steps - 2), steps):
        for e in range(EXAMPLES):
            out_copy(step, e).wait()

    for place in range(chips):
        for piece in kinds:
            core_copy(place * 2 + core, piece).wait_send()
    for far in range(max(rows, chips)):
        for piece in kinds:
            for up in (0, 1):
                if far < rows and piece < steps:
                    origin = me - far if up else me + far

                    @pl.when((origin >= 0) & (me < rows - 1) if up else (origin < rows) & (me > 0))
                    def _():
                        row_copy(origin, piece, up).wait_send()
                if far < chips:
                    source = chip - far if up else chip + far

                    @pl.when((source >= 0) & (chip < chips - 1) if up else (source < chips) & (chip > 0))
                    def _():
                        chip_copy(source, piece, up).wait_send()


def mix_rows(hidden, ids, grad, sign_bits, rows, cols):
    units, tokens = hidden.shape
    depth, columns = tokens * cols, grad.shape[1]
    order = min(units, 256)
    half = sylvester(order)
    anywhere = pl.BlockSpec(memory_space=pl.ANY)
    inside = pl.BlockSpec(memory_space=pltpu.VMEM)
    dma = pltpu.SemaphoreType.DMA
    return pl.pallas_call(
        functools.partial(gather_kernel, rows, cols // 2, order),
        out_shape=jax.ShapeDtypeStruct((EXAMPLES, columns // LANES, units, LANES), jnp.float32),
        in_specs=[inside, inside, inside, anywhere, inside],
        out_specs=anywhere,
        scratch_shapes=[
            pltpu.VMEM((units, depth), jnp.bfloat16),
            pltpu.VMEM((depth, LANES), jnp.bfloat16),
            pltpu.VMEM((depth, columns), jnp.bfloat16),
            pltpu.VMEM((units, columns), jnp.int32),
            pltpu.VMEM((units, WIDE), jnp.float32),
            pltpu.VMEM((units // order, 2 * order, WIDE), jnp.bfloat16),
            pltpu.VMEM((2, EXAMPLES, WIDE // LANES, units, LANES), jnp.float32),
            dma((columns // WIDE,)), dma((2, EXAMPLES)),
            dma((3,)), dma((2, rows, columns // WIDE)), dma((rows, columns // WIDE)),
            dma((2, cols, PIECES + 1)), dma((cols, PIECES + 1)),
            dma((cols, PIECES + 1)), dma((cols, PIECES + 1)),
        ],
        compiler_params=pltpu.CompilerParams(collective_id=0, has_side_effects=True, vmem_limit_bytes=56 << 20),
        name="mix_rows",
    )(hidden, ids, grad, sign_bits, jnp.concatenate([half, half], axis=1))


def reduce_kernel(rows, cols, terms_ref, out_ref, arrived, send_sem, recv_sem):
    me = lax.axis_index("row") * cols + lax.axis_index("col")
    count = rows * cols

    def copy(t):
        target = lax.rem(me + t, count)
        return pltpu.make_async_remote_copy(
            src_ref=terms_ref.at[target], dst_ref=arrived.at[me],
            send_sem=send_sem.at[t], recv_sem=recv_sem.at[t],
            device_id={"row": target // cols, "col": lax.rem(target, cols)}, device_id_type=MESH,
        )

    def greet(t, _):
        target = lax.rem(me + t, count)
        pl.semaphore_signal(
            barrier, inc=1, device_id={"row": target // cols, "col": lax.rem(target, cols)}, device_id_type=MESH
        )
        return 0

    barrier = pltpu.get_barrier_semaphore()
    lax.fori_loop(1, count, greet, 0)
    pl.semaphore_wait(barrier, count - 1)
    lax.fori_loop(1, count, lambda t, _: (copy(t).start(), 0)[1], 0)
    arrived[me] = terms_ref[me]
    lax.fori_loop(1, count, lambda t, _: (copy(t).wait(), 0)[1], 0)
    out_ref[...] = jnp.sum(arrived[...], axis=0)


def reduce(terms, rows, cols):
    return pl.pallas_call(
        functools.partial(reduce_kernel, rows, cols),
        out_shape=jax.ShapeDtypeStruct(terms.shape[1:], jnp.float32),
        in_specs=[pl.BlockSpec(memory_space=pltpu.VMEM)],
        out_specs=pl.BlockSpec(memory_space=pltpu.VMEM),
        scratch_shapes=[
            pltpu.VMEM(terms.shape, jnp.float32),
            pltpu.SemaphoreType.DMA((rows * cols,)),
            pltpu.SemaphoreType.DMA((rows * cols,)),
        ],
        compiler_params=pltpu.CompilerParams(collective_id=1, has_side_effects=True),
        name="reduce",
    )(terms)


def shards(hidden, grad_out, example_ids, sign_bits, sample_index):
    row_block = hidden.shape[1]
    col_block = grad_out.shape[1]
    row_count = lax.axis_size("row")
    col_count = lax.axis_size("col")
    d_total = col_block * col_count
    labels = jnp.broadcast_to(example_ids[:, None], (hidden.shape[0], LANES)).astype(jnp.bfloat16)
    mixed = mix_rows(hidden.T, labels, grad_out, sign_bits, row_count, col_count)
    row_global = sample_index // d_total
    col_global = sample_index % d_total
    row_inner = row_global % row_block
    col_inner = col_global % col_block
    place = (col_inner // LANES) * row_block + row_inner
    low = (col_inner % LANES)[None, :]
    common = jnp.bitwise_count((row_global // row_block) & lax.axis_index("row"))
    common += jnp.bitwise_count((col_global // col_block) & lax.axis_index("col"))
    scale = 1.0 / math.sqrt(row_block * row_count * d_total * TOK_EX)
    weight = jnp.where(common % 2 == 0, scale, -scale).astype(jnp.float32)
    terms = sample(mixed, place, low) * weight[None, :]
    terms = terms.reshape(EXAMPLES, row_count * col_count, -1).transpose(1, 0, 2)
    return reduce(terms, row_count, col_count)


def solution(mesh):
    placed = (
        P(("groups", "col"), "row"),
        P(("groups", "row"), "col"),
        P(("groups", "col")),
        P("row", "col"),
        P(),
    )
    return jax.shard_map(
        shards, mesh=mesh, in_specs=placed, out_specs=P("groups", ("row", "col")), check_vma=False
    )
```
